128 devices in a mesh: vrow: 8 (over y_lo, z), aux: 8 (over x, core), pair: 2 (over y_hi).
Axes of the slice: x: 4, y: 4 (y_hi: 2, y_lo: 2; y = y_hi * 2 + y_lo), z: 4, core: 2. Of those that a mesh axis runs over, the one named last changes fastest.
Arguments:
- factors: bfloat16 [64, 1920, 960], P(('vrow', 'pair'), 'aux'), may hold values from -6 to 6
- amplitudes: bfloat16 [4, 960, 960], replicated, may hold values from -0.00015258789 to 0.00015258789
Outputs:
- ladder: float32 [4, 64, 64], P(None, ('vrow', 'pair'))
The draws below stay inside these ranges and needn't reach their ends.
All inputs are finite; a program needn't handle non-finite values.
Results may differ from the reference program's by a relative error of at most 0.0029.
Values may be sent and summed in bfloat16 or wider, within the bound.
No kernel may reach another device: no remote copies, remote signals or barrier semaphores. Data moves between devices by JAX's collectives and lax.ppermute only.
A program may use at most 192 MiB of HBM per device.

```python
import jax
import jax.numpy as jnp
from jax import lax

V = 960
NAUX = 1920
PAIRS = 4
VW = 64


def level_of(rng, dims, pieces, smallest, largest):
    level, own = 1.0, jax.random.fold_in(rng, 6)
    for dim, blocks in pieces:
        heights = jnp.exp(jax.random.uniform(jax.random.fold_in(own, dim), (blocks,), jnp.float32, smallest / len(pieces), largest / len(pieces)))
        level = level * jnp.repeat(heights, dims[dim] // blocks).reshape([-1 if axis == dim else 1 for axis in range(len(dims))])
    return level


def noise(stream_key, dims, scale, most, split=(), held_as=jnp.bfloat16):
    drawn = scale * jax.random.normal(stream_key, dims, jnp.float32)
    if split:
        drawn = drawn * level_of(stream_key, dims, split, -0.22, 0.18)
    return jnp.clip(drawn, -most, most).astype(held_as)


def setup_inputs(seed: int = 0) -> dict:
    seeds = jax.random.split(jax.random.key(seed), 3)
    factors = noise(seeds[0], (VW, NAUX, V), 1.0, 6.0, ((0, 16), (1, 8)))
    amplitudes = noise(seeds[1], (PAIRS, V, V), (V * V * NAUX) ** -0.5, 0.00015258789)
    return dict(factors=factors, amplitudes=amplitudes)


def reference(factors, amplitudes):
    flat = factors.reshape(VW * NAUX, V)
    right = factors.reshape(VW, NAUX * V)

    def one_pair(amp):
        half = jnp.dot(flat, amp, preferred_element_type=jnp.float32).astype(jnp.bfloat16)
        half = half.reshape(VW, NAUX * V)
        return jnp.dot(half, right.T, preferred_element_type=jnp.float32)

    return lax.map(one_pair, amplitudes)
```

```python
import jax
import jax.numpy as jnp
from jax import lax
from jax.sharding import PartitionSpec as P

ROWS = ("vrow", "pair")


def local(factors, amplitudes):
    mine = lax.all_to_all(factors, ROWS, split_axis=1, concat_axis=0, tiled=True)
    half = jnp.einsum("aqc,pcd->paqd", mine, amplitudes, preferred_element_type=jnp.float32)
    half = half.astype(jnp.bfloat16)
    terms = jnp.einsum("paqd,bqd->pab", half, mine, preferred_element_type=jnp.float32)
    terms = lax.psum_scatter(terms, ROWS, scatter_dimension=1, tiled=True)
    return lax.psum(terms, "aux")


def solution(mesh):
    in_specs = (P(ROWS, "aux", None), P())
    out_specs = P(None, ROWS, None)
    return jax.shard_map(local, mesh=mesh, in_specs=in_specs, out_specs=out_specs, check_vma=False)
```

```python
import functools

import jax
import jax.numpy as jnp
from jax import lax
from jax.experimental import pallas as pl
from jax.experimental.pallas import tpu as pltpu
from jax.sharding import PartitionSpec as P

ROWS = ("vrow", "pair")
ALL = ("vrow", "aux", "pair")
NB = 16
NA = 4
NQ = 15
G = 4
SEND = 64
MIB = 1024 * 1024


def pack_kernel(f_ref, out_ref):
    nq = f_ref.shape[1]
    row = lax.broadcasted_iota(jnp.int32, (SEND, NA * 32), 0)
    col = lax.broadcasted_iota(jnp.int32, (SEND, NA * 32), 1)
    q = (row >> 4) * G + (row & 3)
    a = (row >> 2) & 3
    for j in range(NB):
        base = min(NQ * j // 16 * 16, nq - 32)
        pick = (col == a * 32 + q + (NQ * j - base)) & (q < NQ)
        pick = jnp.where(pick, 1.0, 0.0).astype(jnp.bfloat16)
        window = f_ref[:, base : base + 32, :].reshape(NA * 32, f_ref.shape[2])
        out_ref[j] = jnp.dot(pick, window, preferred_element_type=jnp.float32).astype(jnp.bfloat16)


def ladder_kernel(b_ref, t_ref, out_ref, half_ref, acc_ref):
    p = pl.program_id(0)
    width = b_ref.shape[2]
    rows = b_ref[...].reshape(NB * SEND, width)
    for n in range(0, width, 256):
        m = min(n + 256, width)
        half = jnp.dot(rows, t_ref[0, :, n:m], preferred_element_type=jnp.float32)
        half_ref[:, :, n:m] = half.astype(jnp.bfloat16).reshape(NB, SEND, m - n)

    gram = None
    for g in range(SEND // 16):
        left = half_ref[:, g * 16 : (g + 1) * 16, :].reshape(NB * 16, width)
        right = b_ref[:, g * 16 : (g + 1) * 16, :].reshape(NB * 16, width)
        term = lax.dot_general(left, right, (((1,), (1,)), ((), ())), preferred_element_type=jnp.float32)
        gram = term if gram is None else gram + term

    size = NB * 16
    iota = functools.partial(lax.broadcasted_iota, jnp.int32)
    same = (iota((size, size), 0) & 3) == (iota((size, size), 1) & 3)
    gram = jnp.where(same, gram, 0.0)
    by_b = jnp.where((iota((size, 128), 0) >> 2) + (p // 2) * 64 == iota((size, 128), 1), 1.0, 0.0)
    r, c = iota((128, size), 0), iota((128, size), 1) >> 2
    by_a = jnp.where((c >> 2) * 8 + (p % 2) * 4 + (c & 3) == r, 1.0, 0.0)
    exact = functools.partial(jnp.dot, preferred_element_type=jnp.float32, precision=lax.Precision.HIGHEST)
    part = exact(by_a, exact(gram, by_b))

    @pl.when(p == 0)
    def _():
        acc_ref[...] = part

    @pl.when(p > 0)
    def _():
        acc_ref[...] += part

    @pl.when(p == pl.num_programs(0) - 1)
    def _():
        total = acc_ref[...].reshape(8, 2, 8, 128)
        for x in range(8):
            out_ref[:, x] = total


def sum_kernel(x_ref, out_ref):
    total = jnp.sum(x_ref[...], axis=0)
    for p in range(4):
        out_ref[p] = total[(p % 2) * 4 : (p % 2) * 4 + 4, (p // 2) * 64 : (p // 2) * 64 + 64]


def local(factors, amplitudes):
    width = factors.shape[2]
    npairs = amplitudes.shape[0]
    packed = pl.pallas_call(
        pack_kernel,
        out_shape=jax.ShapeDtypeStruct((NB, SEND, width), jnp.bfloat16),
        compiler_params=pltpu.CompilerParams(vmem_limit_bytes=32 * MIB),
    )(factors)
    mine = lax.all_to_all(packed, ROWS, split_axis=0, concat_axis=0, tiled=True)
    terms = pl.pallas_call(
        ladder_kernel,
        grid=(npairs,),
        in_specs=[
            pl.BlockSpec((NB, SEND, width), lambda p: (0, 0, 0)),
            pl.BlockSpec((1, width, width), lambda p: (p, 0, 0)),
        ],
        out_specs=pl.BlockSpec((8, 8, 2, 8, 128), lambda p: (0, 0, 0, 0, 0)),
        out_shape=jax.ShapeDtypeStruct((8, 8, 2, 8, 128), jnp.float32),
        scratch_shapes=[
            pltpu.VMEM((NB, SEND, width), jnp.bfloat16),
            pltpu.VMEM((128, 128), jnp.float32),
        ],
        compiler_params=pltpu.CompilerParams(vmem_limit_bytes=40 * MIB),
    )(mine, amplitudes)
    terms = lax.all_to_all(terms.reshape(128, 8, 128), ALL, split_axis=0, concat_axis=0, tiled=True)
    return pl.pallas_call(
        sum_kernel,
        out_shape=jax.ShapeDtypeStruct((npairs, NA, NB * NA), jnp.float32),
    )(terms)


def solution(mesh):
    in_specs = (P(ROWS, "aux", None), P())
    out_specs = P(None, ROWS, None)
    return jax.shard_map(local, mesh=mesh, in_specs=in_specs, out_specs=out_specs, check_vma=False)
```

```python
import functools

import jax
import jax.numpy as jnp
from jax import lax
from jax.experimental import pallas as pl
from jax.experimental.pallas import tpu as pltpu
from jax.sharding import PartitionSpec as P

ROWS = ("vrow", "pair")
ALL = ("vrow", "aux", "pair")
V = 960
NB = 16
NA = 4
NQ = 15
G = 4
SEND = 64
MAIN = 896
TILES = MAIN // 128
BLOCK = TILES * SEND + SEND // 2
MIB = 1024 * 1024

iota = functools.partial(lax.broadcasted_iota, jnp.int32)


def pack_kernel(f_ref, out_ref):
    nq = f_ref.shape[1]
    row, col = iota((SEND, NA * 32), 0), iota((SEND, NA * 32), 1)
    q, a = row >> 2, row & 3
    for j in range(NB):
        base = min(NQ * j // 16 * 16, nq - 32)
        pick = (col == a * 32 + q + (NQ * j - base)) & (q < NQ)
        pick = jnp.where(pick, 1.0, 0.0).astype(jnp.bfloat16)
        window = f_ref[:, base : base + 32, :].reshape(NA * 32, V)
        rows = jnp.dot(pick, window, preferred_element_type=jnp.float32).astype(jnp.bfloat16)
        for k in range(TILES):
            out_ref[j, k * SEND : (k + 1) * SEND, :] = rows[:, k * 128 : (k + 1) * 128]
        tails = [rows[: SEND // 2, MAIN:], rows[SEND // 2 :, MAIN:]]
        out_ref[j, TILES * SEND :, :] = jnp.concatenate(tails, axis=1)


def split(x, terms):
    out = []
    for _ in range(terms):
        high = x.astype(jnp.bfloat16)
        out.append(high)
        x = x - high.astype(jnp.float32)
    return out


def ladder_kernel(b_ref, t_ref, out_ref, half_ref, gram_ref, tail_ref):
    npairs = t_ref.shape[0]
    for i in range(npairs // 2):
        tails = [t_ref[2 * i, :, MAIN:], t_ref[2 * i + 1, :, MAIN:]]
        tail_ref[:, i * 128 : (i + 1) * 128] = jnp.concatenate(tails, axis=1)

    def columns(n):
        tiles = []
        for i in (2 * n, 2 * n + 1):
            if i < npairs * TILES:
                tiles.append(t_ref[i // TILES, :, i % TILES * 128 : i % TILES * 128 + 128])
            else:
                i -= npairs * TILES
                tiles.append(tail_ref[:, i * 128 : (i + 1) * 128])
        return jnp.concatenate(tiles, axis=1)

    size = NB * 16
    lane = iota((size, 128), 1)
    for g in range(SEND // 16):
        def block(start):
            return b_ref[:, start : start + 16, :].reshape(size, 128)

        main = jnp.concatenate([block(k * SEND + g * 16) for k in range(TILES)], axis=1)
        low = block(TILES * SEND + g % 2 * 16)
        high = jnp.concatenate([low[:, 64:], low[:, :64]], axis=1)
        if g >= 2:
            low, high = high, low
        low = jnp.where(lane < 64, low, jnp.zeros_like(low))
        high = jnp.where(lane < 64, jnp.zeros_like(high), high)

        rows = jnp.concatenate([main, low[:, :64]], axis=1)
        for n in range(npairs * V // 256):
            half = jnp.dot(rows, columns(n), preferred_element_type=jnp.float32)
            half_ref[g, :, n * 256 : (n + 1) * 256] = half.astype(jnp.bfloat16)

        right = [jnp.concatenate([main, low], axis=1), jnp.concatenate([main, high], axis=1)]
        for p in range(npairs):
            tail = npairs * MAIN + p // 2 * 128
            left = [half_ref[g, :, p * MAIN : (p + 1) * MAIN], half_ref[g, :, tail : tail + 128]]
            term = lax.dot_general(
                jnp.concatenate(left, axis=1),
                right[p % 2],
                (((1,), (1,)), ((), ())),
                preferred_element_type=jnp.float32,
            )
            if g == 0:
                gram_ref[p] = term
            else:
                gram_ref[p] += term

    same = (iota((size, size), 0) >> 2 & 3) == (iota((size, size), 1) >> 2 & 3)
    sums = []
    for p in range(npairs):
        s = jnp.where(same, gram_ref[p], 0.0).reshape(NB, 2, 8, size)
        s = s[:, 0] + s[:, 1]
        sums.append(s + pltpu.roll(s, 4, 1))
    first = iota((NB, 8, size), 1) < 4
    pairs = [jnp.where(first, sums[p], sums[p + 1]).reshape(NB * 8, size) for p in range(0, npairs, 2)]
    r, l = iota((2 * size, 128), 0), iota((2 * size, 128), 1)
    pick = jnp.where(l == (r >> 8) * 64 + (r >> 4 & 15) * 4 + (r & 3), 1.0, 0.0).astype(jnp.bfloat16)
    total = jnp.zeros((NB * 8, 128), jnp.float32)
    for term in split(jnp.concatenate(pairs, axis=1), 3):
        total += jnp.dot(term, pick, preferred_element_type=jnp.float32)
    total = total.reshape(8, 2, 8, 128)
    for x in range(8):
        out_ref[:, x] = total


def sum_kernel(x_ref, out_ref):
    total = jnp.sum(x_ref[...], axis=0)
    for p in range(4):
        out_ref[p] = total[(p % 2) * 4 : (p % 2) * 4 + 4, (p // 2) * 64 : (p // 2) * 64 + 64]


def local(factors, amplitudes):
    npairs = amplitudes.shape[0]
    vmem = pl.BlockSpec(memory_space=pltpu.VMEM)
    packed = pl.pallas_call(
        pack_kernel,
        in_specs=[vmem],
        out_specs=vmem,
        out_shape=jax.ShapeDtypeStruct((NB, BLOCK, 128), jnp.bfloat16),
        compiler_params=pltpu.CompilerParams(vmem_limit_bytes=32 * MIB),
    )(factors)
    mine = lax.all_to_all(packed, ROWS, split_axis=0, concat_axis=0, tiled=True)
    size = NB * 16
    terms = pl.pallas_call(
        ladder_kernel,
        in_specs=[vmem, vmem],
        out_specs=vmem,
        out_shape=jax.ShapeDtypeStruct((8, 8, 2, 8, 128), jnp.float32),
        scratch_shapes=[
            pltpu.VMEM((SEND // 16, size, npairs * V), jnp.bfloat16),
            pltpu.VMEM((npairs, size, size), jnp.float32),
            pltpu.VMEM((V, npairs * 64), jnp.bfloat16),
        ],
        compiler_params=pltpu.CompilerParams(vmem_limit_bytes=40 * MIB),
    )(mine, amplitudes)
    terms = lax.all_to_all(terms.reshape(128, 8, 128), ALL, split_axis=0, concat_axis=0, tiled=True)
    return pl.pallas_call(
        sum_kernel,
        in_specs=[vmem],
        out_specs=vmem,
        out_shape=jax.ShapeDtypeStruct((npairs, NA, NB * NA), jnp.float32),
    )(terms)


def solution(mesh):
    in_specs = (P(ROWS, "aux", None), P())
    out_specs = P(None, ROWS, None)
    return jax.shard_map(local, mesh=mesh, in_specs=in_specs, out_specs=out_specs, check_vma=False)
```

```python
import functools

import jax
import jax.numpy as jnp
from jax import lax
from jax.experimental import pallas as pl
from jax.experimental.pallas import tpu as pltpu
from jax.sharding import PartitionSpec as P

ROWS = ("vrow", "pair")
ALL = ("vrow", "aux", "pair")
V = 960
NB = 16
NA = 4
NQ = 15
G = 4
SEND = 64
MAIN = 896
TILES = MAIN // 128
BLOCK = TILES * SEND + SEND // 2
MIB = 1024 * 1024

iota = functools.partial(lax.broadcasted_iota, jnp.int32)


def pack_kernel(f_ref, out_ref):
    nq = f_ref.shape[1]
    row, col = iota((SEND, NA * 32), 0), iota((SEND, NA * 32), 1)
    q, a = row >> 2, row & 3
    for j in range(NB):
        base = min(NQ * j // 16 * 16, nq - 32)
        pick = (col == a * 32 + q + (NQ * j - base)) & (q < NQ)
        pick = jnp.where(pick, 1.0, 0.0).astype(jnp.bfloat16)
        window = f_ref[:, base : base + 32, :].reshape(NA * 32, V)
        rows = jnp.dot(pick, window, preferred_element_type=jnp.float32).astype(jnp.bfloat16)
        for k in range(TILES):
            out_ref[j, k * SEND : (k + 1) * SEND, :] = rows[:, k * 128 : (k + 1) * 128]
        tails = [rows[: SEND // 2, MAIN:], rows[SEND // 2 :, MAIN:]]
        out_ref[j, TILES * SEND :, :] = jnp.concatenate(tails, axis=1)


def split(x, terms):
    out = []
    for _ in range(terms):
        high = x.astype(jnp.bfloat16)
        out.append(high)
        x = x - high.astype(jnp.float32)
    return out


def ladder_kernel(b_ref, t_ref, out_ref, half_ref, gram_ref, tail_ref):
    npairs = t_ref.shape[0]
    for i in range(npairs // 2):
        tails = [t_ref[2 * i, :, MAIN:], t_ref[2 * i + 1, :, MAIN:]]
        tail_ref[:, i * 128 : (i + 1) * 128] = jnp.concatenate(tails, axis=1)

    def columns(n):
        tiles = []
        for i in (2 * n, 2 * n + 1):
            if i < npairs * TILES:
                tiles.append(t_ref[i // TILES, :, i % TILES * 128 : i % TILES * 128 + 128])
            else:
                i -= npairs * TILES
                tiles.append(tail_ref[:, i * 128 : (i + 1) * 128])
        return jnp.concatenate(tiles, axis=1)

    size = NB * 16
    lane = iota((size, 128), 1)
    for g in range(SEND // 16):
        def block(start):
            return b_ref[:, start : start + 16, :].reshape(size, 128)

        main = jnp.concatenate([block(k * SEND + g * 16) for k in range(TILES)], axis=1)
        low = block(TILES * SEND + g % 2 * 16)
        high = jnp.concatenate([low[:, 64:], low[:, :64]], axis=1)
        if g >= 2:
            low, high = high, low
        low = jnp.where(lane < 64, low, jnp.zeros_like(low))
        high = jnp.where(lane < 64, jnp.zeros_like(high), high)

        rows = jnp.concatenate([main, low[:, :64]], axis=1)
        for n in range(npairs * V // 256):
            half = jnp.dot(rows, columns(n), preferred_element_type=jnp.float32)
            half_ref[g, :, n * 256 : (n + 1) * 256] = half.astype(jnp.bfloat16)

        right = [jnp.concatenate([main, low], axis=1), jnp.concatenate([main, high], axis=1)]
        for p in range(npairs):
            tail = npairs * MAIN + p // 2 * 128
            left = [half_ref[g, :, p * MAIN : (p + 1) * MAIN], half_ref[g, :, tail : tail + 128]]
            term = lax.dot_general(
                jnp.concatenate(left, axis=1),
                right[p % 2],
                (((1,), (1,)), ((), ())),
                preferred_element_type=jnp.float32,
            )
            if g == 0:
                gram_ref[p] = term
            else:
                gram_ref[p] += term

    same = (iota((size, size), 0) >> 2 & 3) == (iota((size, size), 1) >> 2 & 3)
    sums = []
    for p in range(npairs):
        s = jnp.where(same, gram_ref[p], 0.0).reshape(NB, 2, 8, size)
        s = s[:, 0] + s[:, 1]
        sums.append(s + pltpu.roll(s, 4, 1))
    first = iota((NB, 8, size), 1) < 4
    pairs = [jnp.where(first, sums[p], sums[p + 1]).reshape(NB * 8, size) for p in range(0, npairs, 2)]
    r, l = iota((2 * size, 128), 0), iota((2 * size, 128), 1)
    pick = jnp.where(l == (r >> 8) * 64 + (r >> 4 & 15) * 4 + (r & 3), 1.0, 0.0).astype(jnp.bfloat16)
    total = jnp.zeros((NB * 8, 128), jnp.float32)
    for term in split(jnp.concatenate(pairs, axis=1), 3):
        total += jnp.dot(term, pick, preferred_element_type=jnp.float32)
    total = total.reshape(8, 2, 8, 128)
    for x in range(8):
        out_ref[:, x] = total


def sum_kernel(x_ref, out_ref):
    total = jnp.sum(x_ref[...], axis=0)
    for p in range(4):
        out_ref[p] = total[(p % 2) * 4 : (p % 2) * 4 + 4, (p // 2) * 64 : (p // 2) * 64 + 64]


def local(factors, amplitudes):
    npairs = amplitudes.shape[0]
    vmem = pl.BlockSpec(memory_space=pltpu.VMEM)
    packed = pl.pallas_call(
        pack_kernel,
        in_specs=[vmem],
        out_specs=vmem,
        out_shape=jax.ShapeDtypeStruct((NB, BLOCK, 128), jnp.bfloat16),
        compiler_params=pltpu.CompilerParams(vmem_limit_bytes=10 * MIB),
        cost_estimate=pl.CostEstimate(flops=2 * 10**10, bytes_accessed=4 * 10**7, transcendentals=0),
    )(factors)
    mine = lax.all_to_all(packed, ROWS, split_axis=0, concat_axis=0, tiled=True)
    size = NB * 16
    terms = pl.pallas_call(
        ladder_kernel,
        in_specs=[vmem, vmem],
        out_specs=vmem,
        out_shape=jax.ShapeDtypeStruct((8, 8, 2, 8, 128), jnp.float32),
        scratch_shapes=[
            pltpu.VMEM((SEND // 16, size, npairs * V), jnp.bfloat16),
            pltpu.VMEM((npairs, size, size), jnp.float32),
            pltpu.VMEM((V, npairs * 64), jnp.bfloat16),
        ],
        compiler_params=pltpu.CompilerParams(vmem_limit_bytes=28 * MIB),
    )(mine, amplitudes)
    terms = lax.all_to_all(terms.reshape(128, 8, 128), ALL, split_axis=0, concat_axis=0, tiled=True)
    total = jnp.sum(terms, axis=0).reshape(2, NA, npairs // 2, NB * NA)
    return jnp.transpose(total, (2, 0, 1, 3)).reshape(npairs, NA, NB * NA)


def solution(mesh):
    in_specs = (P(ROWS, "aux", None), P())
    out_specs = P(None, ROWS, None)
    return jax.shard_map(local, mesh=mesh, in_specs=in_specs, out_specs=out_specs, check_vma=False)
```

```python
import functools

import jax
import jax.numpy as jnp
from jax import lax
from jax.experimental import pallas as pl
from jax.experimental.pallas import tpu as pltpu
from jax.sharding import PartitionSpec as P

ROWS = ("vrow", "pair")
ALL = ("vrow", "aux", "pair")
V = 960
NB = 16
NA = 4
NQ = 15
G = 4
MAIN = 896
TILES = MAIN // 128
FULL = 3
HEAD = FULL * NA * G
TAIL = TILES * HEAD
LAST = TAIL + 2 * 16
SPREAD = 5
LAST_TILES = [k for k in range(TILES) if k != SPREAD]
BLOCK = LAST + len(LAST_TILES) * 16
MIB = 1024 * 1024

iota = functools.partial(lax.broadcasted_iota, jnp.int32)


def pack_kernel(f_ref, out_ref):
    nq = f_ref.shape[1]
    shape = (HEAD + 3 * 16, NA * 32)
    row, col = iota(shape, 0), iota(shape, 1)
    slot, a = row >> 2 & 3, row & 3
    q = jnp.where(row < HEAD, row >> 2, FULL * G + jnp.where(slot == 3, (row - HEAD) >> 4, slot))
    spread = iota((16, 128), 0) >= 3 * NA
    for j in range(NB):
        base = min(NQ * j // 16 * 16, nq - 32)
        pick = jnp.where(col == a * 32 + q + (NQ * j - base), 1.0, 0.0).astype(jnp.bfloat16)
        window = f_ref[:, base : base + 32, :].reshape(NA * 32, V)
        rows = jnp.dot(pick, window, preferred_element_type=jnp.float32).astype(jnp.bfloat16)

        def tile(start, k):
            return rows[start : start + 16, k * 128 : (k + 1) * 128]

        for k in range(TILES):
            out_ref[j, k * HEAD : (k + 1) * HEAD, :] = rows[:HEAD, k * 128 : (k + 1) * 128]
        for i in range(2):
            tails = [rows[32 * i : 32 * i + 16, MAIN:], rows[32 * i + 16 : 32 * i + 32, MAIN:]]
            out_ref[j, TAIL + 16 * i : TAIL + 16 * i + 16, :] = jnp.concatenate(tails, axis=1)
        for i, k in enumerate(LAST_TILES):
            last = tile(HEAD, k)
            if i < 3:
                last = jnp.where(spread, tile(HEAD + 16 * i, SPREAD), last)
            out_ref[j, LAST + 16 * i : LAST + 16 * i + 16, :] = last


def split(x, terms):
    out = []
    for _ in range(terms):
        high = x.astype(jnp.bfloat16)
        out.append(high)
        x = x - high.astype(jnp.float32)
    return out


def ladder_kernel(b_ref, t_ref, out_ref, half_ref, gram_ref, last_ref, tail_ref):
    npairs = t_ref.shape[0]
    for i in range(npairs // 2):
        tails = [t_ref[2 * i, :, MAIN:], t_ref[2 * i + 1, :, MAIN:]]
        tail_ref[:, i * 128 : (i + 1) * 128] = jnp.concatenate(tails, axis=1)

    def columns(n):
        tiles = []
        for i in (2 * n, 2 * n + 1):
            if i < npairs * TILES:
                tiles.append(t_ref[i // TILES, :, i % TILES * 128 : i % TILES * 128 + 128])
            else:
                i -= npairs * TILES
                tiles.append(tail_ref[:, i * 128 : (i + 1) * 128])
        return jnp.concatenate(tiles, axis=1)

    size = NB * 16
    nlast = 3 * NB * NA

    def block(start):
        return b_ref[:, start : start + 16, :].reshape(size, 128)

    def last_group():
        r, c = iota((nlast, size), 0), iota((nlast, size), 1)
        put = jnp.where(c == (r >> 2 & 15) * 16 + (r >> 6) * 4 + (r & 3), 1.0, 0.0).astype(jnp.bfloat16)
        r, c = iota((NB * NA, size), 0), iota((NB * NA, size), 1)
        get = jnp.where(c == (r >> 2) * 16 + 12 + (r & 3), 1.0, 0.0).astype(jnp.bfloat16)

        def move(matrix, x):
            return jnp.dot(matrix, x, preferred_element_type=jnp.float32).astype(jnp.bfloat16)

        tiles = [block(LAST + 16 * i) for i in range(len(LAST_TILES))]
        spread = [move(get, tiles[i]) for i in range(3)]
        moved = move(put, jnp.concatenate(tiles + [block(TAIL + 16)], axis=1))
        moved = [moved[:, i * 128 : (i + 1) * 128] for i in range(len(LAST_TILES) + 1)]
        moved.insert(SPREAD, jnp.concatenate(spread, axis=0))
        return jnp.concatenate(moved[:TILES], axis=1), moved[TILES]

    for g in range(FULL + 1):
        if g < FULL:
            main = jnp.concatenate([block(k * HEAD + g * 16) for k in range(TILES)], axis=1)
            low = block(TAIL + g // 2 * 16)
        else:
            main, low = last_group()
        nrows = main.shape[0]
        high = jnp.concatenate([low[:, 64:], low[:, :64]], axis=1)
        if g % 2:
            low, high = high, low
        first = iota((nrows, 128), 1) < 64
        low = jnp.where(first, low, jnp.zeros_like(low))
        high = jnp.where(first, jnp.zeros_like(high), high)

        rows = jnp.concatenate([main, low[:, :64]], axis=1)
        for n in range(npairs * V // 256):
            half = jnp.dot(rows, columns(n), preferred_element_type=jnp.float32)
            half_ref[g, :nrows, n * 256 : (n + 1) * 256] = half.astype(jnp.bfloat16)

        right = [jnp.concatenate([main, low], axis=1), jnp.concatenate([main, high], axis=1)]
        for p in range(npairs):
            tail = npairs * MAIN + p // 2 * 128
            left = [half_ref[g, :nrows, p * MAIN : (p + 1) * MAIN], half_ref[g, :nrows, tail : tail + 128]]
            term = lax.dot_general(
                jnp.concatenate(left, axis=1),
                right[p % 2],
                (((1,), (1,)), ((), ())),
                preferred_element_type=jnp.float32,
            )
            if g == 0:
                gram_ref[p] = term
            elif g < FULL:
                gram_ref[p] += term
            else:
                n = NB * NA
                last_ref[p] = term[:n, :n] + term[n : 2 * n, n : 2 * n] + term[2 * n :, 2 * n :]

    same = (iota((size, size), 0) >> 2 & 3) == (iota((size, size), 1) >> 2 & 3)
    sums = []
    for p in range(npairs):
        s = jnp.where(same, gram_ref[p], 0.0).reshape(NB, 2, 8, size)
        s = s[:, 0] + s[:, 1]
        sums.append(s + pltpu.roll(s, 4, 1))
    first = iota((NB, 8, size), 1) < 4
    pairs = [jnp.where(first, sums[p], sums[p + 1]).reshape(NB * 8, size) for p in range(0, npairs, 2)]
    r, l = iota((2 * size, 128), 0), iota((2 * size, 128), 1)
    pick = jnp.where(l == (r >> 8) * 64 + (r >> 4 & 15) * 4 + (r & 3), 1.0, 0.0).astype(jnp.bfloat16)
    total = jnp.zeros((NB * 8, 128), jnp.float32)
    for term in split(jnp.concatenate(pairs, axis=1), 3):
        total += jnp.dot(term, pick, preferred_element_type=jnp.float32)
    total = total.reshape(NB // 2, 2, 8, 128)

    even, odd = [
        jnp.concatenate([last_ref[p], last_ref[p + 2]], axis=1).reshape(NB // 2, 8, 128) for p in range(2)
    ]
    first = iota((NB // 2, 8, 128), 1) < 4
    out_ref[:, 0] = total[:, 0] + jnp.where(first, even, pltpu.roll(odd, 4, 1))
    out_ref[:, 1] = total[:, 1] + jnp.where(first, pltpu.roll(even, 4, 1), odd)


def local(factors, amplitudes):
    npairs = amplitudes.shape[0]
    vmem = pl.BlockSpec(memory_space=pltpu.VMEM)
    packed = pl.pallas_call(
        pack_kernel,
        in_specs=[vmem],
        out_specs=vmem,
        out_shape=jax.ShapeDtypeStruct((NB, BLOCK, 128), jnp.bfloat16),
        compiler_params=pltpu.CompilerParams(vmem_limit_bytes=10 * MIB),
        cost_estimate=pl.CostEstimate(flops=2 * 10**10, bytes_accessed=4 * 10**7, transcendentals=0),
    )(factors)
    mine = lax.all_to_all(packed, ROWS, split_axis=0, concat_axis=0, tiled=True)
    size = NB * 16
    terms = pl.pallas_call(
        ladder_kernel,
        in_specs=[vmem, vmem],
        out_specs=vmem,
        out_shape=jax.ShapeDtypeStruct((NB // 2, 2, 8, 128), jnp.float32),
        scratch_shapes=[
            pltpu.VMEM((FULL + 1, size, npairs * V), jnp.bfloat16),
            pltpu.VMEM((npairs, size, size), jnp.float32),
            pltpu.VMEM((npairs, NB * NA, NB * NA), jnp.float32),
            pltpu.VMEM((V, npairs * 64), jnp.bfloat16),
        ],
        compiler_params=pltpu.CompilerParams(vmem_limit_bytes=28 * MIB),
    )(mine, amplitudes)
    terms = terms + lax.ppermute(terms, "aux", [(i, i ^ 1) for i in range(8)])
    terms = jnp.broadcast_to(terms[:, None], (8, 4, 2, 8, 128)).reshape(64, 8, 128)
    groups = [[(v * 8 + 2 * x + c) * 2 + p for v in range(8) for x in range(4) for p in range(2)] for c in range(2)]
    terms = lax.all_to_all(terms, ALL, split_axis=0, concat_axis=0, tiled=True, axis_index_groups=groups)
    total = jnp.sum(terms, axis=0).reshape(2, NA, npairs // 2, NB * NA)
    return jnp.transpose(total, (2, 0, 1, 3)).reshape(npairs, NA, NB * NA)


def solution(mesh):
    in_specs = (P(ROWS, "aux", None), P())
    out_specs = P(None, ROWS, None)
    return jax.shard_map(local, mesh=mesh, in_specs=in_specs, out_specs=out_specs, check_vma=False)
```

```python
import functools

import jax
import jax.numpy as jnp
from jax import lax
from jax.experimental import pallas as pl
from jax.experimental.pallas import tpu as pltpu
from jax.sharding import PartitionSpec as P

ROWS = ("vrow", "pair")
ALL = ("vrow", "aux", "pair")
V = 960
NB = 16
NA = 4
NQ = 15
G = 4
MAIN = 896
TILES = MAIN // 128
FULL = 3
HEAD = FULL * NA * G
TAIL = TILES * HEAD
LAST = TAIL + 2 * 16
SPREAD = 5
LAST_TILES = [k for k in range(TILES) if k != SPREAD]
BLOCK = LAST + len(LAST_TILES) * 16
MIB = 1024 * 1024

iota = functools.partial(lax.broadcasted_iota, jnp.int32)


def pack_kernel(f_ref, out_ref):
    nq = f_ref.shape[1]
    rows_of = HEAD + 16
    row, col = iota((rows_of, NA * 32), 0), iota((rows_of, NA * 32), 1)
    q, place = row >> 2, (row & 3) * 32
    row, at = iota((3 * 16, NA * 32), 0), iota((3 * 16, NA * 32), 1)
    slot, place4 = FULL * G + (row >> 4), (row & 3) * 32
    fourth = (row & 15) >= 3 * NA
    spread = iota((16, 128), 0) >= 3 * NA
    for j in range(NB):
        base = min(NQ * j // 16 * 16, nq - 32)
        offset = NQ * j - base
        pick = jnp.where((col == place + q + offset) & (q < NQ), 1.0, 0.0).astype(jnp.bfloat16)
        pick4 = jnp.where((at == place4 + slot + offset) & fourth, 1.0, 0.0).astype(jnp.bfloat16)
        window = f_ref[:, base : base + 32, :].reshape(NA * 32, V)
        rows = jnp.dot(pick, window, preferred_element_type=jnp.float32).astype(jnp.bfloat16)
        extra = window[:, SPREAD * 128 : (SPREAD + 1) * 128]
        extra = jnp.dot(pick4, extra, preferred_element_type=jnp.float32).astype(jnp.bfloat16)

        for k in range(TILES):
            out_ref[j, k * HEAD : (k + 1) * HEAD, :] = rows[:HEAD, k * 128 : (k + 1) * 128]
        for i in range(2):
            tails = [rows[32 * i : 32 * i + 16, MAIN:], rows[32 * i + 16 : 32 * i + 32, MAIN:]]
            out_ref[j, TAIL + 16 * i : TAIL + 16 * i + 16, :] = jnp.concatenate(tails, axis=1)
        for i, k in enumerate(LAST_TILES):
            last = rows[HEAD:, k * 128 : (k + 1) * 128]
            if i < 3:
                last = jnp.where(spread, extra[16 * i : 16 * i + 16], last)
            out_ref[j, LAST + 16 * i : LAST + 16 * i + 16, :] = last


def split(x, terms):
    out = []
    for _ in range(terms):
        high = x.astype(jnp.bfloat16)
        out.append(high)
        x = x - high.astype(jnp.float32)
    return out


def ladder_kernel(b_ref, t_ref, out_ref, half_ref, gram_ref, last_ref, tail_ref):
    npairs = t_ref.shape[0]
    for i in range(npairs // 2):
        tails = [t_ref[2 * i, :, MAIN:], t_ref[2 * i + 1, :, MAIN:]]
        tail_ref[:, i * 128 : (i + 1) * 128] = jnp.concatenate(tails, axis=1)

    def columns(n):
        tiles = []
        for i in (2 * n, 2 * n + 1):
            if i < npairs * TILES:
                tiles.append(t_ref[i // TILES, :, i % TILES * 128 : i % TILES * 128 + 128])
            else:
                i -= npairs * TILES
                tiles.append(tail_ref[:, i * 128 : (i + 1) * 128])
        return jnp.concatenate(tiles, axis=1)

    size = NB * 16
    nlast = 3 * NB * NA

    def block(start):
        return b_ref[:, start : start + 16, :].reshape(size, 128)

    def last_group():
        r, c = iota((nlast, size), 0), iota((nlast, size), 1)
        put = jnp.where(c == (r >> 2 & 15) * 16 + (r >> 6) * 4 + (r & 3), 1.0, 0.0).astype(jnp.bfloat16)
        r, c = iota((NB * NA, size), 0), iota((NB * NA, size), 1)
        get = jnp.where(c == (r >> 2) * 16 + 12 + (r & 3), 1.0, 0.0).astype(jnp.bfloat16)

        def move(matrix, x):
            return jnp.dot(matrix, x, preferred_element_type=jnp.float32).astype(jnp.bfloat16)

        tiles = [block(LAST + 16 * i) for i in range(len(LAST_TILES))]
        spread = [move(get, tiles[i]) for i in range(3)]
        moved = move(put, jnp.concatenate(tiles + [block(TAIL + 16)], axis=1))
        moved = [moved[:, i * 128 : (i + 1) * 128] for i in range(len(LAST_TILES) + 1)]
        moved.insert(SPREAD, jnp.concatenate(spread, axis=0))
        return jnp.concatenate(moved[:TILES], axis=1), moved[TILES]

    for g in range(FULL + 1):
        if g < FULL:
            main = jnp.concatenate([block(k * HEAD + g * 16) for k in range(TILES)], axis=1)
            low = block(TAIL + g // 2 * 16)
        else:
            main, low = last_group()
        nrows = main.shape[0]
        high = jnp.concatenate([low[:, 64:], low[:, :64]], axis=1)
        if g % 2:
            low, high = high, low
        first = iota((nrows, 128), 1) < 64
        low = jnp.where(first, low, jnp.zeros_like(low))
        high = jnp.where(first, jnp.zeros_like(high), high)

        rows = jnp.concatenate([main, low[:, :64]], axis=1)
        for n in range(npairs * V // 256):
            half = jnp.dot(rows, columns(n), preferred_element_type=jnp.float32)
            half_ref[g, :nrows, n * 256 : (n + 1) * 256] = half.astype(jnp.bfloat16)

        right = [jnp.concatenate([main, low], axis=1), jnp.concatenate([main, high], axis=1)]
        for p in range(npairs):
            tail = npairs * MAIN + p // 2 * 128
            left = [half_ref[g, :nrows, p * MAIN : (p + 1) * MAIN], half_ref[g, :nrows, tail : tail + 128]]
            term = lax.dot_general(
                jnp.concatenate(left, axis=1),
                right[p % 2],
                (((1,), (1,)), ((), ())),
                preferred_element_type=jnp.float32,
            )
            if g == 0:
                gram_ref[p] = term
            elif g < FULL:
                gram_ref[p] += term
            else:
                n = NB * NA
                last_ref[p] = term[:n, :n] + term[n : 2 * n, n : 2 * n] + term[2 * n :, 2 * n :]

    same = (iota((size, size), 0) >> 2 & 3) == (iota((size, size), 1) >> 2 & 3)
    sums = []
    for p in range(npairs):
        s = jnp.where(same, gram_ref[p], 0.0).reshape(NB, 2, 8, size)
        s = s[:, 0] + s[:, 1]
        sums.append(s + pltpu.roll(s, 4, 1))
    first = iota((NB, 8, size), 1) < 4
    pairs = [jnp.where(first, sums[p], sums[p + 1]).reshape(NB * 8, size) for p in range(0, npairs, 2)]
    r, l = iota((2 * size, 128), 0), iota((2 * size, 128), 1)
    pick = jnp.where(l == (r >> 8) * 64 + (r >> 4 & 15) * 4 + (r & 3), 1.0, 0.0).astype(jnp.bfloat16)
    total = jnp.zeros((NB * 8, 128), jnp.float32)
    for term in split(jnp.concatenate(pairs, axis=1), 3):
        total += jnp.dot(term, pick, preferred_element_type=jnp.float32)
    total = total.reshape(NB // 2, 2, 8, 128)

    even, odd = [
        jnp.concatenate([last_ref[p], last_ref[p + 2]], axis=1).reshape(NB // 2, 8, 128) for p in range(2)
    ]
    first = iota((NB // 2, 8, 128), 1) < 4
    out_ref[:, 0] = total[:, 0] + jnp.where(first, even, pltpu.roll(odd, 4, 1))
    out_ref[:, 1] = total[:, 1] + jnp.where(first, pltpu.roll(even, 4, 1), odd)


def local(factors, amplitudes):
    npairs = amplitudes.shape[0]
    vmem = pl.BlockSpec(memory_space=pltpu.VMEM)
    packed = pl.pallas_call(
        pack_kernel,
        in_specs=[vmem],
        out_specs=vmem,
        out_shape=jax.ShapeDtypeStruct((NB, BLOCK, 128), jnp.bfloat16),
        compiler_params=pltpu.CompilerParams(vmem_limit_bytes=10 * MIB),
        cost_estimate=pl.CostEstimate(flops=2 * 10**10, bytes_accessed=4 * 10**7, transcendentals=0),
    )(factors)
    mine = lax.all_to_all(packed, ROWS, split_axis=0, concat_axis=0, tiled=True)
    size = NB * 16
    terms = pl.pallas_call(
        ladder_kernel,
        in_specs=[vmem, vmem],
        out_specs=vmem,
        out_shape=jax.ShapeDtypeStruct((NB // 2, 2, 8, 128), jnp.float32),
        scratch_shapes=[
            pltpu.VMEM((FULL + 1, size, npairs * V), jnp.bfloat16),
            pltpu.VMEM((npairs, size, size), jnp.float32),
            pltpu.VMEM((npairs, NB * NA, NB * NA), jnp.float32),
            pltpu.VMEM((V, npairs * 64), jnp.bfloat16),
        ],
        compiler_params=pltpu.CompilerParams(vmem_limit_bytes=28 * MIB),
    )(mine, amplitudes)
    terms = terms + lax.ppermute(terms, "aux", [(i, i ^ 1) for i in range(8)])
    terms = terms.astype(jnp.bfloat16)
    terms = jnp.broadcast_to(terms[:, None], (8, 4, 2, 8, 128)).reshape(64, 8, 128)
    groups = [[(v * 8 + 2 * x + c) * 2 + p for v in range(8) for x in range(4) for p in range(2)] for c in range(2)]
    terms = lax.all_to_all(terms, ALL, split_axis=0, concat_axis=0, tiled=True, axis_index_groups=groups)
    total = jnp.sum(terms.astype(jnp.float32), axis=0).reshape(2, NA, npairs // 2, NB * NA)
    return jnp.transpose(total, (2, 0, 1, 3)).reshape(npairs, NA, NB * NA)


def solution(mesh):
    in_specs = (P(ROWS, "aux", None), P())
    out_specs = P(None, ROWS, None)
    return jax.shard_map(local, mesh=mesh, in_specs=in_specs, out_specs=out_specs, check_vma=False)
```

```python
import functools

import jax
import jax.numpy as jnp
from jax import lax
from jax.experimental import pallas as pl
from jax.experimental.pallas import tpu as pltpu
from jax.sharding import PartitionSpec as P

ROWS = ("vrow", "pair")
ALL = ("vrow", "aux", "pair")
V = 960
NB = 16
NA = 4
NQ = 15
G = 4
MAIN = 896
TILES = MAIN // 128
FULL = 3
HEAD = FULL * NA * G
TAIL = TILES * HEAD
LAST = TAIL + 2 * 16
SPREAD = 5
LAST_TILES = [k for k in range(TILES) if k != SPREAD]
BLOCK = LAST + len(LAST_TILES) * 16
MIB = 1024 * 1024

iota = functools.partial(lax.broadcasted_iota, jnp.int32)


def pack_kernel(f_ref, out_ref):
    nq = f_ref.shape[1]
    rows_of = HEAD + 16
    row, col = iota((rows_of, NA * 32), 0), iota((rows_of, NA * 32), 1)
    q, place = row >> 2, (row & 3) * 32
    row, at = iota((3 * 16, NA * 32), 0), iota((3 * 16, NA * 32), 1)
    slot, place4 = FULL * G + (row >> 4), (row & 3) * 32
    fourth = (row & 15) >= 3 * NA
    spread = iota((16, 128), 0) >= 3 * NA
    for j in range(NB):
        base = min(NQ * j // 16 * 16, nq - 32)
        offset = NQ * j - base
        pick = jnp.where((col == place + q + offset) & (q < NQ), 1.0, 0.0).astype(jnp.bfloat16)
        pick4 = jnp.where((at == place4 + slot + offset) & fourth, 1.0, 0.0).astype(jnp.bfloat16)
        window = f_ref[:, base : base + 32, :].reshape(NA * 32, V)
        rows = jnp.dot(pick, window, preferred_element_type=jnp.float32).astype(jnp.bfloat16)
        extra = window[:, SPREAD * 128 : (SPREAD + 1) * 128]
        extra = jnp.dot(pick4, extra, preferred_element_type=jnp.float32).astype(jnp.bfloat16)

        for k in range(TILES):
            out_ref[j, k * HEAD : (k + 1) * HEAD, :] = rows[:HEAD, k * 128 : (k + 1) * 128]
        for i in range(2):
            tails = [rows[32 * i : 32 * i + 16, MAIN:], rows[32 * i + 16 : 32 * i + 32, MAIN:]]
            out_ref[j, TAIL + 16 * i : TAIL + 16 * i + 16, :] = jnp.concatenate(tails, axis=1)
        for i, k in enumerate(LAST_TILES):
            last = rows[HEAD:, k * 128 : (k + 1) * 128]
            if i < 3:
                last = jnp.where(spread, extra[16 * i : 16 * i + 16], last)
            out_ref[j, LAST + 16 * i : LAST + 16 * i + 16, :] = last


def split(x, terms):
    out = []
    for _ in range(terms):
        high = x.astype(jnp.bfloat16)
        out.append(high)
        x = x - high.astype(jnp.float32)
    return out


def ladder_kernel(b_ref, t_ref, out_ref, half_ref, gram_ref, last_ref, tail_ref):
    npairs = t_ref.shape[0]
    for i in range(npairs // 2):
        tails = [t_ref[2 * i, :, MAIN:], t_ref[2 * i + 1, :, MAIN:]]
        tail_ref[:, i * 128 : (i + 1) * 128] = jnp.concatenate(tails, axis=1)

    def columns(n):
        tiles = []
        for i in (2 * n, 2 * n + 1):
            if i < npairs * TILES:
                tiles.append(t_ref[i // TILES, :, i % TILES * 128 : i % TILES * 128 + 128])
            else:
                i -= npairs * TILES
                tiles.append(tail_ref[:, i * 128 : (i + 1) * 128])
        return jnp.concatenate(tiles, axis=1)

    size = NB * 16
    nlast = 3 * NB * NA

    def block(start):
        return b_ref[:, start : start + 16, :].reshape(size, 128)

    def last_group():
        r, c = iota((nlast, size), 0), iota((nlast, size), 1)
        put = jnp.where(c == (NB - 1 - (r >> 2 & 15)) * 16 + (r >> 6) * 4 + (r & 3), 1.0, 0.0).astype(jnp.bfloat16)
        r, c = iota((NB * NA, size), 0), iota((NB * NA, size), 1)
        get = jnp.where(c == (NB - 1 - (r >> 2)) * 16 + 12 + (r & 3), 1.0, 0.0).astype(jnp.bfloat16)

        def move(matrix, x):
            return jnp.dot(matrix, x, preferred_element_type=jnp.float32).astype(jnp.bfloat16)

        tiles = [block(LAST + 16 * i) for i in range(len(LAST_TILES))]
        spread = [move(get, tiles[i]) for i in range(3)]
        moved = move(put, jnp.concatenate(tiles + [block(TAIL + 16)], axis=1))
        moved = [moved[:, i * 128 : (i + 1) * 128] for i in range(len(LAST_TILES) + 1)]
        moved.insert(SPREAD, jnp.concatenate(spread, axis=0))
        return jnp.concatenate(moved[:TILES], axis=1), moved[TILES]

    for g in range(FULL + 1):
        if g < FULL:
            main = jnp.concatenate([block(k * HEAD + g * 16) for k in range(TILES)], axis=1)
            low = block(TAIL + g // 2 * 16)
        else:
            main, low = last_group()
        nrows = main.shape[0]
        high = jnp.concatenate([low[:, 64:], low[:, :64]], axis=1)
        if g % 2:
            low, high = high, low
        first = iota((nrows, 128), 1) < 64
        low = jnp.where(first, low, jnp.zeros_like(low))
        high = jnp.where(first, jnp.zeros_like(high), high)

        rows = jnp.concatenate([main, low[:, :64]], axis=1)
        for n in range(npairs * V // 256):
            half = jnp.dot(rows, columns(n), preferred_element_type=jnp.float32)
            half_ref[g, :nrows, n * 256 : (n + 1) * 256] = half.astype(jnp.bfloat16)

        right = [jnp.concatenate([main, low], axis=1), jnp.concatenate([main, high], axis=1)]
        for p in range(npairs):
            tail = npairs * MAIN + p // 2 * 128
            left = [half_ref[g, :nrows, p * MAIN : (p + 1) * MAIN], half_ref[g, :nrows, tail : tail + 128]]
            term = lax.dot_general(
                jnp.concatenate(left, axis=1),
                right[p % 2],
                (((1,), (1,)), ((), ())),
                preferred_element_type=jnp.float32,
            )
            if g == 0:
                gram_ref[p] = term
            elif g < FULL:
                gram_ref[p] += term
            else:
                n = NB * NA
                last_ref[p] = term[:n, :n] + term[n : 2 * n, n : 2 * n] + term[2 * n :, 2 * n :]

    same = (iota((size, size), 0) >> 2 & 3) == (iota((size, size), 1) >> 2 & 3)
    sums = []
    for p in range(npairs):
        s = jnp.where(same, gram_ref[p], 0.0).reshape(NB, 2, 8, size)
        s = s[:, 0] + s[:, 1]
        sums.append(s + pltpu.roll(s, 4, 1))
    first = iota((NB, 8, size), 1) < 4
    pairs = [jnp.where(first, sums[p], sums[p + 1]).reshape(NB * 8, size) for p in range(0, npairs, 2)]
    r, l = iota((2 * size, 128), 0), iota((2 * size, 128), 1)
    pick = jnp.where(l == (r >> 8) * 64 + (NB - 1 - (r >> 4 & 15)) * 4 + (r & 3), 1.0, 0.0).astype(jnp.bfloat16)
    total = jnp.zeros((NB * 8, 128), jnp.float32)
    for term in split(jnp.concatenate(pairs, axis=1), 3):
        total += jnp.dot(term, pick, preferred_element_type=jnp.float32)
    total = total.reshape(NB // 2, 2, 8, 128)

    even, odd = [
        jnp.concatenate([last_ref[p], last_ref[p + 2]], axis=1).reshape(NB // 2, 8, 128) for p in range(2)
    ]
    first = iota((NB // 2, 8, 128), 1) < 4
    even, odd = [
        jnp.where(first, even, pltpu.roll(odd, 4, 1)),
        jnp.where(first, pltpu.roll(even, 4, 1), odd),
    ]
    for m in range(NB // 2):
        out_ref[m, 0] = total[m, 0] + odd[NB // 2 - 1 - m]
        out_ref[m, 1] = total[m, 1] + even[NB // 2 - 1 - m]


def local(factors, amplitudes):
    npairs = amplitudes.shape[0]
    vmem = pl.BlockSpec(memory_space=pltpu.VMEM)
    packed = pl.pallas_call(
        pack_kernel,
        in_specs=[vmem],
        out_specs=vmem,
        out_shape=jax.ShapeDtypeStruct((NB, BLOCK, 128), jnp.bfloat16),
        compiler_params=pltpu.CompilerParams(vmem_limit_bytes=10 * MIB),
        cost_estimate=pl.CostEstimate(flops=2 * 10**10, bytes_accessed=4 * 10**7, transcendentals=0),
    )(factors)
    groups = [[(v * 8 + x) * 2 + p for v in range(8) for p in range(2)][::-1] for x in range(8)]
    mine = lax.all_to_all(packed, ALL, split_axis=0, concat_axis=0, tiled=True, axis_index_groups=groups)
    size = NB * 16
    terms = pl.pallas_call(
        ladder_kernel,
        in_specs=[vmem, vmem],
        out_specs=vmem,
        out_shape=jax.ShapeDtypeStruct((NB // 2, 2, 8, 128), jnp.float32),
        scratch_shapes=[
            pltpu.VMEM((FULL + 1, size, npairs * V), jnp.bfloat16),
            pltpu.VMEM((npairs, size, size), jnp.float32),
            pltpu.VMEM((npairs, NB * NA, NB * NA), jnp.float32),
            pltpu.VMEM((V, npairs * 64), jnp.bfloat16),
        ],
        compiler_params=pltpu.CompilerParams(vmem_limit_bytes=28 * MIB),
    )(mine, amplitudes)
    terms = terms + lax.ppermute(terms, "aux", [(i, i ^ 1) for i in range(8)])
    terms = terms.astype(jnp.bfloat16)
    terms = jnp.broadcast_to(terms[:, None], (8, 4, 2, 8, 128)).reshape(64, 8, 128)
    groups = [
        [(v * 8 + 2 * x + c) * 2 + p for v in range(8) for x in range(4) for p in range(2)][::-1] for c in range(2)
    ]
    terms = lax.all_to_all(terms, ALL, split_axis=0, concat_axis=0, tiled=True, axis_index_groups=groups)
    total = jnp.sum(terms.astype(jnp.float32), axis=0).reshape(2, NA, npairs // 2, NB * NA)
    return jnp.transpose(total, (2, 0, 1, 3)).reshape(npairs, NA, NB * NA)


def solution(mesh):
    in_specs = (P(ROWS, "aux", None), P())
    out_specs = P(None, ROWS, None)
    return jax.shard_map(local, mesh=mesh, in_specs=in_specs, out_specs=out_specs, check_vma=False)
```

```python
import functools

import jax
import jax.numpy as jnp
from jax import lax
from jax.experimental import pallas as pl
from jax.experimental.pallas import tpu as pltpu
from jax.sharding import PartitionSpec as P

ROWS = ("vrow", "pair")
ALL = ("vrow", "aux", "pair")
V = 960
NB = 16
VROWS = (2, 7, 6, 5, 4, 3, 1, 0)
XS = (2, 3, 1, 0)
PAIRS = (1, 0)
NA = 4
NQ = 15
G = 4
MAIN = 896
TILES = MAIN // 128
FULL = 3
HEAD = FULL * NA * G
TAIL = TILES * HEAD
LAST = TAIL + 2 * 16
SPREAD = 5
LAST_TILES = [k for k in range(TILES) if k != SPREAD]
BLOCK = LAST + len(LAST_TILES) * 16
MIB = 1024 * 1024

iota = functools.partial(lax.broadcasted_iota, jnp.int32)


def pack_kernel(f_ref, out_ref):
    nq = f_ref.shape[1]
    rows_of = HEAD + 16
    row, col = iota((rows_of, NA * 32), 0), iota((rows_of, NA * 32), 1)
    q, place = row >> 2, (row & 3) * 32
    row, at = iota((3 * 16, NA * 32), 0), iota((3 * 16, NA * 32), 1)
    slot, place4 = FULL * G + (row >> 4), (row & 3) * 32
    fourth = (row & 15) >= 3 * NA
    spread = iota((16, 128), 0) >= 3 * NA
    for j in range(NB):
        base = min(NQ * j // 16 * 16, nq - 32)
        offset = NQ * j - base
        pick = jnp.where((col == place + q + offset) & (q < NQ), 1.0, 0.0).astype(jnp.bfloat16)
        pick4 = jnp.where((at == place4 + slot + offset) & fourth, 1.0, 0.0).astype(jnp.bfloat16)
        window = f_ref[:, base : base + 32, :].reshape(NA * 32, V)
        rows = jnp.dot(pick, window, preferred_element_type=jnp.float32).astype(jnp.bfloat16)
        extra = window[:, SPREAD * 128 : (SPREAD + 1) * 128]
        extra = jnp.dot(pick4, extra, preferred_element_type=jnp.float32).astype(jnp.bfloat16)

        for k in range(TILES):
            out_ref[j, k * HEAD : (k + 1) * HEAD, :] = rows[:HEAD, k * 128 : (k + 1) * 128]
        for i in range(2):
            tails = [rows[32 * i : 32 * i + 16, MAIN:], rows[32 * i + 16 : 32 * i + 32, MAIN:]]
            out_ref[j, TAIL + 16 * i : TAIL + 16 * i + 16, :] = jnp.concatenate(tails, axis=1)
        for i, k in enumerate(LAST_TILES):
            last = rows[HEAD:, k * 128 : (k + 1) * 128]
            if i < 3:
                last = jnp.where(spread, extra[16 * i : 16 * i + 16], last)
            out_ref[j, LAST + 16 * i : LAST + 16 * i + 16, :] = last


def split(x, terms):
    out = []
    for _ in range(terms):
        high = x.astype(jnp.bfloat16)
        out.append(high)
        x = x - high.astype(jnp.float32)
    return out


def ladder_kernel(b_ref, t_ref, out_ref, half_ref, gram_ref, last_ref, tail_ref):
    npairs = t_ref.shape[0]
    for i in range(npairs // 2):
        tails = [t_ref[2 * i, :, MAIN:], t_ref[2 * i + 1, :, MAIN:]]
        tail_ref[:, i * 128 : (i + 1) * 128] = jnp.concatenate(tails, axis=1)

    def columns(n):
        tiles = []
        for i in (2 * n, 2 * n + 1):
            if i < npairs * TILES:
                tiles.append(t_ref[i // TILES, :, i % TILES * 128 : i % TILES * 128 + 128])
            else:
                i -= npairs * TILES
                tiles.append(tail_ref[:, i * 128 : (i + 1) * 128])
        return jnp.concatenate(tiles, axis=1)

    size = NB * 16
    nlast = 3 * NB * NA

    def block(start):
        return b_ref[:, start : start + 16, :].reshape(size, 128)

    def last_group():
        r, c = iota((nlast, size), 0), iota((nlast, size), 1)
        put = jnp.where(c == (NB - 1 - (r >> 2 & 15)) * 16 + (r >> 6) * 4 + (r & 3), 1.0, 0.0).astype(jnp.bfloat16)
        r, c = iota((NB * NA, size), 0), iota((NB * NA, size), 1)
        get = jnp.where(c == (NB - 1 - (r >> 2)) * 16 + 12 + (r & 3), 1.0, 0.0).astype(jnp.bfloat16)

        def move(matrix, x):
            return jnp.dot(matrix, x, preferred_element_type=jnp.float32).astype(jnp.bfloat16)

        tiles = [block(LAST + 16 * i) for i in range(len(LAST_TILES))]
        spread = [move(get, tiles[i]) for i in range(3)]
        moved = move(put, jnp.concatenate(tiles + [block(TAIL + 16)], axis=1))
        moved = [moved[:, i * 128 : (i + 1) * 128] for i in range(len(LAST_TILES) + 1)]
        moved.insert(SPREAD, jnp.concatenate(spread, axis=0))
        return jnp.concatenate(moved[:TILES], axis=1), moved[TILES]

    for g in range(FULL + 1):
        if g < FULL:
            main = jnp.concatenate([block(k * HEAD + g * 16) for k in range(TILES)], axis=1)
            low = block(TAIL + g // 2 * 16)
        else:
            main, low = last_group()
        nrows = main.shape[0]
        high = jnp.concatenate([low[:, 64:], low[:, :64]], axis=1)
        if g % 2:
            low, high = high, low
        first = iota((nrows, 128), 1) < 64
        low = jnp.where(first, low, jnp.zeros_like(low))
        high = jnp.where(first, jnp.zeros_like(high), high)

        rows = jnp.concatenate([main, low[:, :64]], axis=1)
        for n in range(npairs * V // 256):
            half = jnp.dot(rows, columns(n), preferred_element_type=jnp.float32)
            half_ref[g, :nrows, n * 256 : (n + 1) * 256] = half.astype(jnp.bfloat16)

        right = [jnp.concatenate([main, low], axis=1), jnp.concatenate([main, high], axis=1)]
        for p in range(npairs):
            tail = npairs * MAIN + p // 2 * 128
            left = [half_ref[g, :nrows, p * MAIN : (p + 1) * MAIN], half_ref[g, :nrows, tail : tail + 128]]
            term = lax.dot_general(
                jnp.concatenate(left, axis=1),
                right[p % 2],
                (((1,), (1,)), ((), ())),
                preferred_element_type=jnp.float32,
            )
            if g == 0:
                gram_ref[p] = term
            elif g < FULL:
                gram_ref[p] += term
            else:
                n = NB * NA
                last_ref[p] = term[:n, :n] + term[n : 2 * n, n : 2 * n] + term[2 * n :, 2 * n :]

    same = (iota((size, size), 0) >> 2 & 3) == (iota((size, size), 1) >> 2 & 3)
    sums = []
    for p in range(npairs):
        s = jnp.where(same, gram_ref[p], 0.0).reshape(NB, 2, 8, size)
        s = s[:, 0] + s[:, 1]
        sums.append(s + pltpu.roll(s, 4, 1))
    first = iota((NB, 8, size), 1) < 4
    pairs = [jnp.where(first, sums[p], sums[p + 1]).reshape(NB * 8, size) for p in range(0, npairs, 2)]
    r, l = iota((2 * size, 128), 0), iota((2 * size, 128), 1)
    pick = jnp.where(l == (r >> 8) * 64 + (NB - 1 - (r >> 4 & 15)) * 4 + (r & 3), 1.0, 0.0).astype(jnp.bfloat16)
    total = jnp.zeros((NB * 8, 128), jnp.float32)
    for term in split(jnp.concatenate(pairs, axis=1), 3):
        total += jnp.dot(term, pick, preferred_element_type=jnp.float32)
    total = total.reshape(NB // 2, 2, 8, 128)

    even, odd = [
        jnp.concatenate([last_ref[p], last_ref[p + 2]], axis=1).reshape(NB // 2, 8, 128) for p in range(2)
    ]
    first = iota((NB // 2, 8, 128), 1) < 4
    even, odd = [
        jnp.where(first, even, pltpu.roll(odd, 4, 1)),
        jnp.where(first, pltpu.roll(even, 4, 1), odd),
    ]
    for device in range(NB):
        v, p, at = device // 2, device % 2, NB - 1 - device
        out_ref[VROWS.index(v), PAIRS.index(p)] = total[at // 2, at % 2] + (odd if p else even)[v]


def local(factors, amplitudes):
    npairs = amplitudes.shape[0]
    vmem = pl.BlockSpec(memory_space=pltpu.VMEM)
    packed = pl.pallas_call(
        pack_kernel,
        in_specs=[vmem],
        out_specs=vmem,
        out_shape=jax.ShapeDtypeStruct((NB, BLOCK, 128), jnp.bfloat16),
        compiler_params=pltpu.CompilerParams(vmem_limit_bytes=10 * MIB),
        cost_estimate=pl.CostEstimate(flops=2 * 10**10, bytes_accessed=4 * 10**7, transcendentals=0),
    )(factors)
    groups = [[(v * 8 + x) * 2 + p for v in range(8) for p in range(2)][::-1] for x in range(8)]
    mine = lax.all_to_all(packed, ALL, split_axis=0, concat_axis=0, tiled=True, axis_index_groups=groups)
    size = NB * 16
    terms = pl.pallas_call(
        ladder_kernel,
        in_specs=[vmem, vmem],
        out_specs=vmem,
        out_shape=jax.ShapeDtypeStruct((NB // 2, 2, 8, 128), jnp.float32),
        scratch_shapes=[
            pltpu.VMEM((FULL + 1, size, npairs * V), jnp.bfloat16),
            pltpu.VMEM((npairs, size, size), jnp.float32),
            pltpu.VMEM((npairs, NB * NA, NB * NA), jnp.float32),
            pltpu.VMEM((V, npairs * 64), jnp.bfloat16),
        ],
        compiler_params=pltpu.CompilerParams(vmem_limit_bytes=28 * MIB),
    )(mine, amplitudes)
    terms = terms + lax.ppermute(terms, "aux", [(i, i ^ 1) for i in range(8)])
    terms = terms.astype(jnp.bfloat16)
    terms = jnp.broadcast_to(terms[:, None], (8, 4, 2, 8, 128)).reshape(64, 8, 128)
    groups = [[(v * 8 + 2 * x + c) * 2 + p for v in VROWS for x in XS for p in PAIRS] for c in range(2)]
    terms = lax.all_to_all(terms, ALL, split_axis=0, concat_axis=0, tiled=True, axis_index_groups=groups)
    total = jnp.sum(terms.astype(jnp.float32), axis=0).reshape(2, NA, npairs // 2, NB * NA)
    return jnp.transpose(total, (2, 0, 1, 3)).reshape(npairs, NA, NB * NA)


def solution(mesh):
    in_specs = (P(ROWS, "aux", None), P())
    out_specs = P(None, ROWS, None)
    return jax.shard_map(local, mesh=mesh, in_specs=in_specs, out_specs=out_specs, check_vma=False)
```

```python
import functools

import jax
import jax.numpy as jnp
from jax import lax
from jax.experimental import pallas as pl
from jax.experimental.pallas import tpu as pltpu
from jax.sharding import PartitionSpec as P

ROWS = ("vrow", "pair")
ALL = ("vrow", "aux", "pair")
V = 960
NB = 16
VROWS = (2, 7, 6, 5, 4, 3, 1, 0)
XS = (2, 3, 1, 0)
PAIRS = (1, 0)
NA = 4
NQ = 15
G = 4
MAIN = 896
TILES = MAIN // 128
FULL = 3
HEAD = FULL * NA * G
TAIL = TILES * HEAD
LAST = TAIL + 2 * 16
SPREAD = 5
LAST_TILES = [k for k in range(TILES) if k != SPREAD]
BLOCK = LAST + len(LAST_TILES) * 16
MIB = 1024 * 1024

iota = functools.partial(lax.broadcasted_iota, jnp.int32)


def pack_kernel(f_ref, out_ref):
    nq = f_ref.shape[1]
    rows_of = HEAD + 16
    row, col = iota((rows_of, NA * 32), 0), iota((rows_of, NA * 32), 1)
    q, place = row >> 2, (row & 3) * 32
    row, at = iota((3 * 16, NA * 32), 0), iota((3 * 16, NA * 32), 1)
    slot, place4 = FULL * G + (row >> 4), (row & 3) * 32
    fourth = (row & 15) >= 3 * NA
    spread = iota((16, 128), 0) >= 3 * NA
    for j in range(NB):
        base = min(NQ * j // 16 * 16, nq - 32)
        offset = NQ * j - base
        pick = jnp.where((col == place + q + offset) & (q < NQ), 1.0, 0.0).astype(jnp.bfloat16)
        pick4 = jnp.where((at == place4 + slot + offset) & fourth, 1.0, 0.0).astype(jnp.bfloat16)
        window = f_ref[:, base : base + 32, :].reshape(NA * 32, V)
        rows = jnp.dot(pick, window, preferred_element_type=jnp.float32).astype(jnp.bfloat16)
        extra = window[:, SPREAD * 128 : (SPREAD + 1) * 128]
        extra = jnp.dot(pick4, extra, preferred_element_type=jnp.float32).astype(jnp.bfloat16)

        for k in range(TILES):
            out_ref[j, k * HEAD : (k + 1) * HEAD, :] = rows[:HEAD, k * 128 : (k + 1) * 128]
        for i in range(2):
            tails = [rows[32 * i : 32 * i + 16, MAIN:], rows[32 * i + 16 : 32 * i + 32, MAIN:]]
            out_ref[j, TAIL + 16 * i : TAIL + 16 * i + 16, :] = jnp.concatenate(tails, axis=1)
        for i, k in enumerate(LAST_TILES):
            last = rows[HEAD:, k * 128 : (k + 1) * 128]
            if i < 3:
                last = jnp.where(spread, extra[16 * i : 16 * i + 16], last)
            out_ref[j, LAST + 16 * i : LAST + 16 * i + 16, :] = last


def split(x, terms):
    out = []
    for _ in range(terms):
        high = x.astype(jnp.bfloat16)
        out.append(high)
        x = x - high.astype(jnp.float32)
    return out


def ladder_kernel(b_ref, t_ref, out_ref, half_ref, gram_ref, last_ref, tail_ref):
    npairs = t_ref.shape[0]
    for i in range(npairs // 2):
        tails = [t_ref[2 * i, :, MAIN:], t_ref[2 * i + 1, :, MAIN:]]
        tail_ref[:, i * 128 : (i + 1) * 128] = jnp.concatenate(tails, axis=1)

    def columns(n):
        tiles = []
        for i in (2 * n, 2 * n + 1):
            if i < npairs * TILES:
                tiles.append(t_ref[i // TILES, :, i % TILES * 128 : i % TILES * 128 + 128])
            else:
                i -= npairs * TILES
                tiles.append(tail_ref[:, i * 128 : (i + 1) * 128])
        return jnp.concatenate(tiles, axis=1)

    size = NB * 16
    nlast = 3 * NB * NA

    def block(start):
        return b_ref[:, start : start + 16, :].reshape(size, 128)

    def last_group():
        r, c = iota((nlast, size), 0), iota((nlast, size), 1)
        put = jnp.where(c == (NB - 1 - (r >> 2 & 15)) * 16 + (r >> 6) * 4 + (r & 3), 1.0, 0.0).astype(jnp.bfloat16)
        r, c = iota((NB * NA, size), 0), iota((NB * NA, size), 1)
        get = jnp.where(c == (NB - 1 - (r >> 2)) * 16 + 12 + (r & 3), 1.0, 0.0).astype(jnp.bfloat16)

        def move(matrix, x):
            return jnp.dot(matrix, x, preferred_element_type=jnp.float32).astype(jnp.bfloat16)

        tiles = [block(LAST + 16 * i) for i in range(len(LAST_TILES))]
        spread = [move(get, tiles[i]) for i in range(3)]
        moved = move(put, jnp.concatenate(tiles + [block(TAIL + 16)], axis=1))
        moved = [moved[:, i * 128 : (i + 1) * 128] for i in range(len(LAST_TILES) + 1)]
        moved.insert(SPREAD, jnp.concatenate(spread, axis=0))
        return jnp.concatenate(moved[:TILES], axis=1), moved[TILES]

    for g in range(FULL + 1):
        if g < FULL:
            main = jnp.concatenate([block(k * HEAD + g * 16) for k in range(TILES)], axis=1)
            low = block(TAIL + g // 2 * 16)
        else:
            main, low = last_group()
        nrows = main.shape[0]
        high = jnp.concatenate([low[:, 64:], low[:, :64]], axis=1)
        if g % 2:
            low, high = high, low
        first = iota((nrows, 128), 1) < 64
        low = jnp.where(first, low, jnp.zeros_like(low))
        high = jnp.where(first, jnp.zeros_like(high), high)

        rows = jnp.concatenate([main, low[:, :64]], axis=1)
        for n in range(npairs * V // 256):
            half = jnp.dot(rows, columns(n), preferred_element_type=jnp.float32)
            half_ref[g, :nrows, n * 256 : (n + 1) * 256] = half.astype(jnp.bfloat16)

        right = [jnp.concatenate([main, low], axis=1), jnp.concatenate([main, high], axis=1)]
        for p in range(npairs):
            tail = npairs * MAIN + p // 2 * 128
            left = [half_ref[g, :nrows, p * MAIN : (p + 1) * MAIN], half_ref[g, :nrows, tail : tail + 128]]
            term = lax.dot_general(
                jnp.concatenate(left, axis=1),
                right[p % 2],
                (((1,), (1,)), ((), ())),
                preferred_element_type=jnp.float32,
            )
            if g == 0:
                gram_ref[p] = term
            elif g < FULL:
                gram_ref[p] += term
            else:
                n = NB * NA
                last_ref[p] = term[:n, :n] + term[n : 2 * n, n : 2 * n] + term[2 * n :, 2 * n :]

    same = (iota((size, size), 0) >> 2 & 3) == (iota((size, size), 1) >> 2 & 3)
    sums = []
    for p in range(npairs):
        s = jnp.where(same, gram_ref[p], 0.0).reshape(NB, 2, 8, size)
        s = s[:, 0] + s[:, 1]
        sums.append(s + pltpu.roll(s, 4, 1))
    first = iota((NB, 8, size), 1) < 4
    pairs = [jnp.where(first, sums[p], sums[p + 1]).reshape(NB * 8, size) for p in range(0, npairs, 2)]
    r, l = iota((2 * size, 128), 0), iota((2 * size, 128), 1)
    pick = jnp.where(l == (r >> 8) * 64 + (NB - 1 - (r >> 4 & 15)) * 4 + (r & 3), 1.0, 0.0).astype(jnp.bfloat16)
    total = jnp.zeros((NB * 8, 128), jnp.float32)
    for term in split(jnp.concatenate(pairs, axis=1), 3):
        total += jnp.dot(term, pick, preferred_element_type=jnp.float32)
    total = total.reshape(NB // 2, 2, 8, 128)

    even, odd = [
        jnp.concatenate([last_ref[p], last_ref[p + 2]], axis=1).reshape(NB // 2, 8, 128) for p in range(2)
    ]
    first = iota((NB // 2, 8, 128), 1) < 4
    even, odd = [
        jnp.where(first, even, pltpu.roll(odd, 4, 1)),
        jnp.where(first, pltpu.roll(even, 4, 1), odd),
    ]
    for device in range(NB):
        v, p, at = device // 2, device % 2, NB - 1 - device
        out_ref[VROWS.index(v), PAIRS.index(p)] = total[at // 2, at % 2] + (odd if p else even)[v]


def local(factors, amplitudes):
    npairs = amplitudes.shape[0]
    vmem = pl.BlockSpec(memory_space=pltpu.VMEM)
    packed = pl.pallas_call(
        pack_kernel,
        in_specs=[vmem],
        out_specs=vmem,
        out_shape=jax.ShapeDtypeStruct((NB, BLOCK, 128), jnp.bfloat16),
        compiler_params=pltpu.CompilerParams(vmem_limit_bytes=10 * MIB),
        cost_estimate=pl.CostEstimate(flops=2 * 10**10, bytes_accessed=4 * 10**7, transcendentals=0),
    )(factors)
    groups = [[(v * 8 + x) * 2 + p for v in range(8) for p in range(2)][::-1] for x in range(8)]
    mine = lax.all_to_all(packed, ALL, split_axis=0, concat_axis=0, tiled=True, axis_index_groups=groups)
    size = NB * 16
    terms = pl.pallas_call(
        ladder_kernel,
        in_specs=[vmem, vmem],
        out_specs=vmem,
        out_shape=jax.ShapeDtypeStruct((NB // 2, 2, 8, 128), jnp.float32),
        scratch_shapes=[
            pltpu.VMEM((FULL + 1, size, npairs * V), jnp.bfloat16),
            pltpu.VMEM((npairs, size, size), jnp.float32),
            pltpu.VMEM((npairs, NB * NA, NB * NA), jnp.float32),
            pltpu.VMEM((V, npairs * 64), jnp.bfloat16),
        ],
        compiler_params=pltpu.CompilerParams(vmem_limit_bytes=28 * MIB),
    )(mine, amplitudes)
    terms = terms + lax.ppermute(terms, "aux", [(i, i ^ 1) for i in range(8)])
    terms = jnp.broadcast_to(terms[:, None], (8, 4, 2, 8, 128)).reshape(64, 8, 128)
    groups = [[(v * 8 + 2 * x + c) * 2 + p for v in VROWS for x in XS for p in PAIRS] for c in range(2)]
    terms = lax.all_to_all(terms, ALL, split_axis=0, concat_axis=0, tiled=True, axis_index_groups=groups)
    total = jnp.sum(terms, axis=0).reshape(2, NA, npairs // 2, NB * NA)
    return jnp.transpose(total, (2, 0, 1, 3)).reshape(npairs, NA, NB * NA)


def solution(mesh):
    in_specs = (P(ROWS, "aux", None), P())
    out_specs = P(None, ROWS, None)
    return jax.shard_map(local, mesh=mesh, in_specs=in_specs, out_specs=out_specs, check_vma=False)
```

```python
import functools

import jax
import jax.numpy as jnp
from jax import lax
from jax.experimental import pallas as pl
from jax.experimental.pallas import tpu as pltpu
from jax.sharding import PartitionSpec as P

ROWS = ("vrow", "pair")
ALL = ("vrow", "aux", "pair")
V = 960
NB = 16
VROWS = (2, 7, 6, 5, 4, 3, 1, 0)
XS = (2, 3, 1, 0)
PAIRS = (1, 0)
NA = 4
NQ = 15
G = 4
MAIN = 896
TILES = MAIN // 128
FULL = 3
HEAD = FULL * NA * G
TAIL = TILES * HEAD
LAST = TAIL + 2 * 16
SPREAD = 5
LAST_TILES = [k for k in range(TILES) if k != SPREAD]
BLOCK = LAST + len(LAST_TILES) * 16
MIB = 1024 * 1024

iota = functools.partial(lax.broadcasted_iota, jnp.int32)


def pack_kernel(f_ref, out_ref):
    nq = f_ref.shape[1]
    rows_of = HEAD + 16
    row, col = iota((rows_of, NA * 32), 0), iota((rows_of, NA * 32), 1)
    q, place = row >> 2, (row & 3) * 32
    row, at = iota((3 * 16, NA * 32), 0), iota((3 * 16, NA * 32), 1)
    slot, place4 = FULL * G + (row >> 4), (row & 3) * 32
    fourth = (row & 15) >= 3 * NA
    spread = iota((16, 128), 0) >= 3 * NA
    for j in range(NB):
        base = min(NQ * j // 16 * 16, nq - 32)
        offset = NQ * j - base
        pick = jnp.where((col == place + q + offset) & (q < NQ), 1.0, 0.0).astype(jnp.bfloat16)
        pick4 = jnp.where((at == place4 + slot + offset) & fourth, 1.0, 0.0).astype(jnp.bfloat16)
        window = f_ref[:, base : base + 32, :].reshape(NA * 32, V)
        rows = jnp.dot(pick, window, preferred_element_type=jnp.float32).astype(jnp.bfloat16)
        extra = window[:, SPREAD * 128 : (SPREAD + 1) * 128]
        extra = jnp.dot(pick4, extra, preferred_element_type=jnp.float32).astype(jnp.bfloat16)

        for k in range(TILES):
            out_ref[j, k * HEAD : (k + 1) * HEAD, :] = rows[:HEAD, k * 128 : (k + 1) * 128]
        for i in range(2):
            tails = [rows[32 * i : 32 * i + 16, MAIN:], rows[32 * i + 16 : 32 * i + 32, MAIN:]]
            out_ref[j, TAIL + 16 * i : TAIL + 16 * i + 16, :] = jnp.concatenate(tails, axis=1)
        for i, k in enumerate(LAST_TILES):
            last = rows[HEAD:, k * 128 : (k + 1) * 128]
            if i < 3:
                last = jnp.where(spread, extra[16 * i : 16 * i + 16], last)
            out_ref[j, LAST + 16 * i : LAST + 16 * i + 16, :] = last


def split(x, terms):
    out = []
    for _ in range(terms):
        high = x.astype(jnp.bfloat16)
        out.append(high)
        x = x - high.astype(jnp.float32)
    return out


def ladder_kernel(b_ref, t_ref, out_ref, half_ref, gram_ref, last_ref, tail_ref):
    npairs = t_ref.shape[0]
    for i in range(npairs // 2):
        tails = [t_ref[2 * i, :, MAIN:], t_ref[2 * i + 1, :, MAIN:]]
        tail_ref[:, i * 128 : (i + 1) * 128] = jnp.concatenate(tails, axis=1)

    def columns(n):
        tiles = []
        for i in (2 * n, 2 * n + 1):
            if i < npairs * TILES:
                tiles.append(t_ref[i // TILES, :, i % TILES * 128 : i % TILES * 128 + 128])
            else:
                i -= npairs * TILES
                tiles.append(tail_ref[:, i * 128 : (i + 1) * 128])
        return jnp.concatenate(tiles, axis=1)

    size = NB * 16
    nlast = 3 * NB * NA

    def block(start):
        return b_ref[:, start : start + 16, :].reshape(size, 128)

    def last_group():
        r, c = iota((nlast, size), 0), iota((nlast, size), 1)
        put = jnp.where(c == (NB - 1 - (r >> 2 & 15)) * 16 + (r >> 6) * 4 + (r & 3), 1.0, 0.0).astype(jnp.bfloat16)
        r, c = iota((NB * NA, size), 0), iota((NB * NA, size), 1)
        get = jnp.where(c == (NB - 1 - (r >> 2)) * 16 + 12 + (r & 3), 1.0, 0.0).astype(jnp.bfloat16)

        def move(matrix, x):
            return jnp.dot(matrix, x, preferred_element_type=jnp.float32).astype(jnp.bfloat16)

        tiles = [block(LAST + 16 * i) for i in range(len(LAST_TILES))]
        spread = [move(get, tiles[i]) for i in range(3)]
        moved = move(put, jnp.concatenate(tiles + [block(TAIL + 16)], axis=1))
        moved = [moved[:, i * 128 : (i + 1) * 128] for i in range(len(LAST_TILES) + 1)]
        moved.insert(SPREAD, jnp.concatenate(spread, axis=0))
        return jnp.concatenate(moved[:TILES], axis=1), moved[TILES]

    for g in range(FULL + 1):
        if g < FULL:
            main = jnp.concatenate([block(k * HEAD + g * 16) for k in range(TILES)], axis=1)
            low = block(TAIL + g // 2 * 16)
        else:
            main, low = last_group()
        nrows = main.shape[0]
        high = jnp.concatenate([low[:, 64:], low[:, :64]], axis=1)
        if g % 2:
            low, high = high, low
        first = iota((nrows, 128), 1) < 64
        low = jnp.where(first, low, jnp.zeros_like(low))
        high = jnp.where(first, jnp.zeros_like(high), high)

        rows = jnp.concatenate([main, low[:, :64]], axis=1)
        for n in range(npairs * V // 256):
            half = jnp.dot(rows, columns(n), preferred_element_type=jnp.float32)
            half_ref[g, :nrows, n * 256 : (n + 1) * 256] = half.astype(jnp.bfloat16)

        right = [jnp.concatenate([main, low], axis=1), jnp.concatenate([main, high], axis=1)]
        for p in range(npairs):
            tail = npairs * MAIN + p // 2 * 128
            left = [half_ref[g, :nrows, p * MAIN : (p + 1) * MAIN], half_ref[g, :nrows, tail : tail + 128]]
            term = lax.dot_general(
                jnp.concatenate(left, axis=1),
                right[p % 2],
                (((1,), (1,)), ((), ())),
                preferred_element_type=jnp.float32,
            )
            if g == 0:
                gram_ref[p] = term
            elif g < FULL:
                gram_ref[p] += term
            else:
                n = NB * NA
                last_ref[p] = term[:n, :n] + term[n : 2 * n, n : 2 * n] + term[2 * n :, 2 * n :]

    same = (iota((size, size), 0) >> 2 & 3) == (iota((size, size), 1) >> 2 & 3)
    sums = []
    for p in range(npairs):
        s = jnp.where(same, gram_ref[p], 0.0).reshape(NB, 2, 8, size)
        s = s[:, 0] + s[:, 1]
        sums.append(s + pltpu.roll(s, 4, 1))
    first = iota((NB, 8, size), 1) < 4
    pairs = [jnp.where(first, sums[p], sums[p + 1]).reshape(NB * 8, size) for p in range(0, npairs, 2)]
    r, l = iota((2 * size, 128), 0), iota((2 * size, 128), 1)
    pick = jnp.where(l == (r >> 8) * 64 + (NB - 1 - (r >> 4 & 15)) * 4 + (r & 3), 1.0, 0.0).astype(jnp.bfloat16)
    total = jnp.zeros((NB * 8, 128), jnp.float32)
    for term in split(jnp.concatenate(pairs, axis=1), 2):
        total += jnp.dot(term, pick, preferred_element_type=jnp.float32)
    total = total.reshape(NB // 2, 2, 8, 128)

    even, odd = [
        jnp.concatenate([last_ref[p], last_ref[p + 2]], axis=1).reshape(NB // 2, 8, 128) for p in range(2)
    ]
    first = iota((NB // 2, 8, 128), 1) < 4
    even, odd = [
        jnp.where(first, even, pltpu.roll(odd, 4, 1)),
        jnp.where(first, pltpu.roll(even, 4, 1), odd),
    ]
    for device in range(NB):
        v, p, at = device // 2, device % 2, NB - 1 - device
        out_ref[VROWS.index(v), PAIRS.index(p)] = total[at // 2, at % 2] + (odd if p else even)[v]


def local(factors, amplitudes):
    npairs = amplitudes.shape[0]
    vmem = pl.BlockSpec(memory_space=pltpu.VMEM)
    packed = pl.pallas_call(
        pack_kernel,
        in_specs=[vmem],
        out_specs=vmem,
        out_shape=jax.ShapeDtypeStruct((NB, BLOCK, 128), jnp.bfloat16),
        compiler_params=pltpu.CompilerParams(vmem_limit_bytes=10 * MIB),
        cost_estimate=pl.CostEstimate(flops=2 * 10**10, bytes_accessed=4 * 10**7, transcendentals=0),
    )(factors)
    groups = [[(v * 8 + x) * 2 + p for v in range(8) for p in range(2)][::-1] for x in range(8)]
    mine = lax.all_to_all(packed, ALL, split_axis=0, concat_axis=0, tiled=True, axis_index_groups=groups)
    size = NB * 16
    terms = pl.pallas_call(
        ladder_kernel,
        in_specs=[vmem, vmem],
        out_specs=vmem,
        out_shape=jax.ShapeDtypeStruct((NB // 2, 2, 8, 128), jnp.float32),
        scratch_shapes=[
            pltpu.VMEM((FULL + 1, size, npairs * V), jnp.bfloat16),
            pltpu.VMEM((npairs, size, size), jnp.float32),
            pltpu.VMEM((npairs, NB * NA, NB * NA), jnp.float32),
            pltpu.VMEM((V, npairs * 64), jnp.bfloat16),
        ],
        compiler_params=pltpu.CompilerParams(vmem_limit_bytes=28 * MIB),
    )(mine, amplitudes)
    terms = terms + lax.ppermute(terms, "aux", [(i, i ^ 1) for i in range(8)])
    terms = terms.astype(jnp.bfloat16)
    terms = jnp.broadcast_to(terms[:, None], (8, 4, 2, 8, 128)).reshape(64, 8, 128)
    groups = [[(v * 8 + 2 * x + c) * 2 + p for v in VROWS for x in XS for p in PAIRS] for c in range(2)]
    terms = lax.all_to_all(terms, ALL, split_axis=0, concat_axis=0, tiled=True, axis_index_groups=groups)
    total = jnp.sum(terms.astype(jnp.float32), axis=0).reshape(2, NA, npairs // 2, NB * NA)
    return jnp.transpose(total, (2, 0, 1, 3)).reshape(npairs, NA, NB * NA)


def solution(mesh):
    in_specs = (P(ROWS, "aux", None), P())
    out_specs = P(None, ROWS, None)
    return jax.shard_map(local, mesh=mesh, in_specs=in_specs, out_specs=out_specs, check_vma=False)
```

```python
import functools

import jax
import jax.numpy as jnp
from jax import lax
from jax.experimental import pallas as pl
from jax.experimental.pallas import tpu as pltpu
from jax.sharding import PartitionSpec as P

ROWS = ("vrow", "pair")
ALL = ("vrow", "aux", "pair")
V = 960
NB = 16
VROWS = (2, 0, 1, 3, 4, 5, 6, 7)
XS = (2, 0, 1, 3)
PAIRS = (1, 0)
NA = 4
NQ = 15
G = 4
MAIN = 896
TILES = MAIN // 128
FULL = 3
HEAD = FULL * NA * G
TAIL = TILES * HEAD
LAST = TAIL + 2 * 16
SPREAD = 5
LAST_TILES = [k for k in range(TILES) if k != SPREAD]
BLOCK = LAST + len(LAST_TILES) * 16
MIB = 1024 * 1024

iota = functools.partial(lax.broadcasted_iota, jnp.int32)


def pack_kernel(f_ref, out_ref):
    nq = f_ref.shape[1]
    rows_of = HEAD + 16
    row, col = iota((rows_of, NA * 32), 0), iota((rows_of, NA * 32), 1)
    q, place = row >> 2, (row & 3) * 32
    row, at = iota((3 * 16, NA * 32), 0), iota((3 * 16, NA * 32), 1)
    slot, place4 = FULL * G + (row >> 4), (row & 3) * 32
    fourth = (row & 15) >= 3 * NA
    spread = iota((16, 128), 0) >= 3 * NA
    for j in range(NB):
        base = min(NQ * j // 16 * 16, nq - 32)
        offset = NQ * j - base
        pick = jnp.where((col == place + q + offset) & (q < NQ), 1.0, 0.0).astype(jnp.bfloat16)
        pick4 = jnp.where((at == place4 + slot + offset) & fourth, 1.0, 0.0).astype(jnp.bfloat16)
        window = f_ref[:, base : base + 32, :].reshape(NA * 32, V)
        rows = jnp.dot(pick, window, preferred_element_type=jnp.float32).astype(jnp.bfloat16)
        extra = window[:, SPREAD * 128 : (SPREAD + 1) * 128]
        extra = jnp.dot(pick4, extra, preferred_element_type=jnp.float32).astype(jnp.bfloat16)

        for k in range(TILES):
            out_ref[j, k * HEAD : (k + 1) * HEAD, :] = rows[:HEAD, k * 128 : (k + 1) * 128]
        for i in range(2):
            tails = [rows[32 * i : 32 * i + 16, MAIN:], rows[32 * i + 16 : 32 * i + 32, MAIN:]]
            out_ref[j, TAIL + 16 * i : TAIL + 16 * i + 16, :] = jnp.concatenate(tails, axis=1)
        for i, k in enumerate(LAST_TILES):
            last = rows[HEAD:, k * 128 : (k + 1) * 128]
            if i < 3:
                last = jnp.where(spread, extra[16 * i : 16 * i + 16], last)
            out_ref[j, LAST + 16 * i : LAST + 16 * i + 16, :] = last


def split(x, terms):
    out = []
    for _ in range(terms):
        high = x.astype(jnp.bfloat16)
        out.append(high)
        x = x - high.astype(jnp.float32)
    return out


def ladder_kernel(b_ref, t_ref, out_ref, half_ref, gram_ref, last_ref, tail_ref):
    npairs = t_ref.shape[0]
    for i in range(npairs // 2):
        tails = [t_ref[2 * i, :, MAIN:], t_ref[2 * i + 1, :, MAIN:]]
        tail_ref[:, i * 128 : (i + 1) * 128] = jnp.concatenate(tails, axis=1)

    def columns(n):
        tiles = []
        for i in (2 * n, 2 * n + 1):
            if i < npairs * TILES:
                tiles.append(t_ref[i // TILES, :, i % TILES * 128 : i % TILES * 128 + 128])
            else:
                i -= npairs * TILES
                tiles.append(tail_ref[:, i * 128 : (i + 1) * 128])
        return jnp.concatenate(tiles, axis=1)

    size = NB * 16
    nlast = 3 * NB * NA

    def block(start):
        return b_ref[:, start : start + 16, :].reshape(size, 128)

    def last_group():
        r, c = iota((nlast, size), 0), iota((nlast, size), 1)
        put = jnp.where(c == (NB - 1 - (r >> 2 & 15)) * 16 + (r >> 6) * 4 + (r & 3), 1.0, 0.0).astype(jnp.bfloat16)
        r, c = iota((NB * NA, size), 0), iota((NB * NA, size), 1)
        get = jnp.where(c == (NB - 1 - (r >> 2)) * 16 + 12 + (r & 3), 1.0, 0.0).astype(jnp.bfloat16)

        def move(matrix, x):
            return jnp.dot(matrix, x, preferred_element_type=jnp.float32).astype(jnp.bfloat16)

        tiles = [block(LAST + 16 * i) for i in range(len(LAST_TILES))]
        spread = [move(get, tiles[i]) for i in range(3)]
        moved = move(put, jnp.concatenate(tiles + [block(TAIL + 16)], axis=1))
        moved = [moved[:, i * 128 : (i + 1) * 128] for i in range(len(LAST_TILES) + 1)]
        moved.insert(SPREAD, jnp.concatenate(spread, axis=0))
        return jnp.concatenate(moved[:TILES], axis=1), moved[TILES]

    for g in range(FULL + 1):
        if g < FULL:
            main = jnp.concatenate([block(k * HEAD + g * 16) for k in range(TILES)], axis=1)
            low = block(TAIL + g // 2 * 16)
        else:
            main, low = last_group()
        nrows = main.shape[0]
        high = jnp.concatenate([low[:, 64:], low[:, :64]], axis=1)
        if g % 2:
            low, high = high, low
        first = iota((nrows, 128), 1) < 64
        low = jnp.where(first, low, jnp.zeros_like(low))
        high = jnp.where(first, jnp.zeros_like(high), high)

        rows = jnp.concatenate([main, low[:, :64]], axis=1)
        for n in range(npairs * V // 256):
            half = jnp.dot(rows, columns(n), preferred_element_type=jnp.float32)
            half_ref[g, :nrows, n * 256 : (n + 1) * 256] = half.astype(jnp.bfloat16)

        right = [jnp.concatenate([main, low], axis=1), jnp.concatenate([main, high], axis=1)]
        for p in range(npairs):
            tail = npairs * MAIN + p // 2 * 128
            left = [half_ref[g, :nrows, p * MAIN : (p + 1) * MAIN], half_ref[g, :nrows, tail : tail + 128]]
            term = lax.dot_general(
                jnp.concatenate(left, axis=1),
                right[p % 2],
                (((1,), (1,)), ((), ())),
                preferred_element_type=jnp.float32,
            )
            if g == 0:
                gram_ref[p] = term
            elif g < FULL:
                gram_ref[p] += term
            else:
                n = NB * NA
                last_ref[p] = term[:n, :n] + term[n : 2 * n, n : 2 * n] + term[2 * n :, 2 * n :]

    same = (iota((size, size), 0) >> 2 & 3) == (iota((size, size), 1) >> 2 & 3)
    sums = []
    for p in range(npairs):
        s = jnp.where(same, gram_ref[p], 0.0).reshape(NB, 2, 8, size)
        s = s[:, 0] + s[:, 1]
        sums.append(s + pltpu.roll(s, 4, 1))
    first = iota((NB, 8, size), 1) < 4
    pairs = [jnp.where(first, sums[p], sums[p + 1]).reshape(NB * 8, size) for p in range(0, npairs, 2)]
    r, l = iota((2 * size, 128), 0), iota((2 * size, 128), 1)
    pick = jnp.where(l == (r >> 8) * 64 + (NB - 1 - (r >> 4 & 15)) * 4 + (r & 3), 1.0, 0.0).astype(jnp.bfloat16)
    total = jnp.zeros((NB * 8, 128), jnp.float32)
    for term in split(jnp.concatenate(pairs, axis=1), 3):
        total += jnp.dot(term, pick, preferred_element_type=jnp.float32)
    total = total.reshape(NB // 2, 2, 8, 128)

    even, odd = [
        jnp.concatenate([last_ref[p], last_ref[p + 2]], axis=1).reshape(NB // 2, 8, 128) for p in range(2)
    ]
    first = iota((NB // 2, 8, 128), 1) < 4
    even, odd = [
        jnp.where(first, even, pltpu.roll(odd, 4, 1)),
        jnp.where(first, pltpu.roll(even, 4, 1), odd),
    ]
    for device in range(NB):
        v, p, at = device // 2, device % 2, NB - 1 - device
        out_ref[VROWS.index(v), PAIRS.index(p)] = total[at // 2, at % 2] + (odd if p else even)[v]


def local(factors, amplitudes):
    npairs = amplitudes.shape[0]
    vmem = pl.BlockSpec(memory_space=pltpu.VMEM)
    packed = pl.pallas_call(
        pack_kernel,
        in_specs=[vmem],
        out_specs=vmem,
        out_shape=jax.ShapeDtypeStruct((NB, BLOCK, 128), jnp.bfloat16),
        compiler_params=pltpu.CompilerParams(vmem_limit_bytes=10 * MIB),
        cost_estimate=pl.CostEstimate(flops=2 * 10**10, bytes_accessed=4 * 10**7, transcendentals=0),
    )(factors)
    groups = [[(v * 8 + x) * 2 + p for v in range(8) for p in range(2)][::-1] for x in range(8)]
    mine = lax.all_to_all(packed, ALL, split_axis=0, concat_axis=0, tiled=True, axis_index_groups=groups)
    size = NB * 16
    terms = pl.pallas_call(
        ladder_kernel,
        in_specs=[vmem, vmem],
        out_specs=vmem,
        out_shape=jax.ShapeDtypeStruct((NB // 2, 2, 8, 128), jnp.float32),
        scratch_shapes=[
            pltpu.VMEM((FULL + 1, size, npairs * V), jnp.bfloat16),
            pltpu.VMEM((npairs, size, size), jnp.float32),
            pltpu.VMEM((npairs, NB * NA, NB * NA), jnp.float32),
            pltpu.VMEM((V, npairs * 64), jnp.bfloat16),
        ],
        compiler_params=pltpu.CompilerParams(vmem_limit_bytes=28 * MIB),
    )(mine, amplitudes)
    terms = terms + lax.ppermute(terms, "aux", [(i, i ^ 1) for i in range(8)])
    terms = terms.astype(jnp.bfloat16)
    terms = jnp.broadcast_to(terms[:, None], (8, 4, 2, 8, 128)).reshape(64, 8, 128)
    groups = [[(v * 8 + 2 * x + c) * 2 + p for v in VROWS for x in XS for p in PAIRS] for c in range(2)]
    terms = lax.all_to_all(terms, ALL, split_axis=0, concat_axis=0, tiled=True, axis_index_groups=groups)
    total = jnp.sum(terms.astype(jnp.float32), axis=0).reshape(2, NA, npairs // 2, NB * NA)
    return jnp.transpose(total, (2, 0, 1, 3)).reshape(npairs, NA, NB * NA)


def solution(mesh):
    in_specs = (P(ROWS, "aux", None), P())
    out_specs = P(None, ROWS, None)
    return jax.shard_map(local, mesh=mesh, in_specs=in_specs, out_specs=out_specs, check_vma=False)
```
